256 devices in a mesh: blk: 64 (over x, z, core), op: 4 (over y).
Axes of the slice: x: 4, y: 4, z: 8, core: 2. Of those that a mesh axis runs over, the one named last changes fastest.
Arguments:
- wavefunction: bfloat16 [384, 16, 128, 128], P('blk'), may hold values from -6 to 6
- left_env: bfloat16 [16, 384, 128, 128], P('op', 'blk'), may hold values from -0.5 to 0.5
- right_env: bfloat16 [16, 384, 128, 128], P('op', 'blk'), may hold values from -0.125 to 0.125
- left_dims: int32 [384], replicated, may hold values from 32 to 128, as said below
- right_dims: int32 [384], replicated, may hold values from 32 to 128, as said below
- partner: int32 [384, 16], replicated, may hold values from 0 to 383, as said below
Outputs:
- hpsi: bfloat16 [384, 16, 128, 128], P('blk', None, 'op')
The draws below stay inside these ranges and needn't reach their ends.
Inputs may be any that keep to these rules, and one draw needn't show every extreme that they name: `left_dims`: true dimension of a left block; some block has the full 128. `right_dims`: true dimension of a right block; some block has the full 128. `partner`: right block j lies on index j // 6 of blk; the 16 partners of one left block are distinct; the tiles of the left blocks of one index of blk have at most 2 partners on any one index of blk, and exactly 2 on some index, and some index of blk holds 2 partners of the tiles of every index.
All inputs are finite; a program needn't handle non-finite values.
Results may differ from the reference program's by a relative error of at most 0.005.
Values may be sent and summed in bfloat16 or wider, within the bound.
No kernel may reach another device: no remote copies, remote signals or barrier semaphores. Data moves between devices by JAX's collectives and lax.ppermute only.
A program may use at most 128 MiB of HBM per device.

```python
import jax
import jax.numpy as jnp
from jax import lax

S = 128
PAIRS = 16
SEC_DEV = 6
NSEC = 384
KW = 16
CAP = 2
N_BLK = 64


def sector_dims(key, number):
    key_dims, key_spot = jax.random.split(key)
    drawn_dims = jax.random.randint(key_dims, (number,), S // 4, S)
    full_spot = jax.random.randint(key_spot, (), 0, number)
    return jnp.where(jnp.arange(number) == full_spot, S, drawn_dims).astype(jnp.int32)


def draw_left_dims(key, part):
    key = jax.random.fold_in(key, 11)
    return sector_dims(key, NSEC)


def draw_right_dims(key, part):
    key = jax.random.fold_in(key, 23)
    return sector_dims(key, NSEC)


def draw_partner(key, part):
    key = jax.random.fold_in(key, 37)
    key_order, key_offset, key_shift, key_left, key_pair = jax.random.split(key, 5)
    hot_order = jax.random.permutation(key_order, N_BLK).astype(jnp.int32)
    offsets = jax.random.randint(key_offset, (N_BLK,), 0, N_BLK - 1)
    step_ids = jnp.arange(N_BLK, dtype=jnp.int32)
    rotated = hot_order[1 + (step_ids[None, :] - 1 + offsets[:, None]) % (N_BLK - 1)]
    owner_order = jnp.where(step_ids[None, :] == 0, hot_order[0], rotated)
    slot_ids = jnp.arange(SEC_DEV * PAIRS, dtype=jnp.int32)
    owner_step = slot_ids // CAP
    slot_within = slot_ids % CAP
    owners = owner_order[:, owner_step]
    shifts = jax.random.randint(key_shift, (N_BLK, N_BLK), 0, SEC_DEV)
    shift_here = jnp.take_along_axis(shifts, owners, axis=1)
    local_index = (slot_within[None, :] + slot_within[None, :] // SEC_DEV + shift_here) % SEC_DEV
    right_global = owners * SEC_DEV + local_index
    left_perm = jax.vmap(lambda one_key: jax.random.permutation(one_key, SEC_DEV))(jax.random.split(key_left, N_BLK))
    pair_perm = jax.vmap(lambda one_key: jax.random.permutation(one_key, PAIRS))(jax.random.split(key_pair, N_BLK * SEC_DEV))
    pair_perm = pair_perm.reshape(N_BLK, SEC_DEV, PAIRS)
    raw_left = slot_ids % SEC_DEV
    raw_pair = slot_ids // SEC_DEV
    new_left = left_perm[:, raw_left]
    new_pair = pair_perm[:, raw_left, raw_pair]
    device_ids = jnp.broadcast_to(step_ids[:, None], new_left.shape)
    partner_table = jnp.zeros((N_BLK, SEC_DEV, PAIRS), jnp.int32)
    partner_table = partner_table.at[device_ids, new_left, new_pair].set(right_global.astype(jnp.int32))
    return partner_table.reshape(NSEC, PAIRS).astype(jnp.int32)


def block_scale(key, dims, cuts, smallest, high):
    gain, own = 1.0, jax.random.fold_in(key, 6)
    for axis_at, blocks in cuts:
        heights = jnp.exp(jax.random.uniform(jax.random.fold_in(own, axis_at), (blocks,), jnp.float32, smallest / len(cuts), high / len(cuts)))
        gain = gain * jnp.repeat(heights, dims[axis_at] // blocks).reshape([-1 if axis == axis_at else 1 for axis in range(len(dims))])
    return gain


def gaussian(stream_key, dims, spread, reach, cuts=(), kind=jnp.bfloat16):
    array = spread * jax.random.normal(stream_key, dims, jnp.float32)
    if cuts:
        array = array * block_scale(stream_key, dims, cuts, -0.22, 0.18)
    return jnp.clip(array, -reach, reach).astype(kind)


def setup_inputs(seed: int = 0) -> dict:
    arg_keys = jax.random.split(jax.random.key(seed), 7)
    return {
        "wavefunction": gaussian(arg_keys[0], (NSEC, PAIRS, S, S), 1.0, 6.0, ((0, 64),)),
        "left_env": gaussian(arg_keys[1], (KW, NSEC, S, S), S ** -0.5, 0.5, ((0, 4), (1, 64))),
        "right_env": gaussian(arg_keys[2], (KW, NSEC, S, S), (S * KW) ** -0.5, 0.125, ((0, 4), (1, 64))),
        "left_dims": draw_left_dims(jax.random.fold_in(arg_keys[6], 71), 0),
        "right_dims": draw_right_dims(jax.random.fold_in(arg_keys[6], 71), 0),
        "partner": draw_partner(jax.random.fold_in(arg_keys[6], 71), 0),
    }


def reference(wavefunction, left_env, right_env, left_dims, right_dims, partner):
    row_ids = jnp.arange(S, dtype=jnp.int32)
    partner_dims = jnp.take(right_dims, partner.astype(jnp.int32), axis=0)
    row_mask = (row_ids[None, :] < left_dims[:, None]).astype(jnp.bfloat16)
    column_mask = (row_ids[None, None, :] < partner_dims[:, :, None]).astype(jnp.bfloat16)
    masked = wavefunction * row_mask[:, None, :, None] * column_mask[:, :, None, :]
    left_terms = jnp.transpose(left_env, (1, 0, 2, 3))

    def one_block(pieces):
        psi_block, left_blocks, partners_here, row_weights, column_weights = pieces
        product = jnp.einsum("tab,pbc->tpac", left_blocks.astype(jnp.float32), psi_block.astype(jnp.float32))
        product = lax.optimization_barrier(product.astype(jnp.bfloat16)).astype(jnp.float32)
        right_blocks = jnp.take(right_env, partners_here.astype(jnp.int32), axis=1).astype(jnp.float32)
        summed = jnp.einsum("tpab,tpcb->pac", product, right_blocks)
        summed = summed * row_weights.astype(jnp.float32)[None, :, None] * column_weights.astype(jnp.float32)[:, None, :]
        return summed.astype(jnp.bfloat16)

    return lax.map(one_block, (masked, left_terms, partner, row_mask, column_mask))
```

```python
import functools

import jax
import jax.numpy as jnp
from jax import lax
from jax.experimental import pallas as pl
from jax.experimental.pallas import tpu as pltpu
from jax.sharding import Mesh
from jax.sharding import PartitionSpec as P

STEPS = (0, 1, -1, 2, -2, 3, -3, 4)
CHUNKS = ((0, 3), (3, 5), (5, 8))
CAP = 2


def shift(array, axis, by):
    count = lax.axis_size(axis)
    return lax.ppermute(array, axis, [(i, (i + by) % count) for i in range(count)])


def both_ways(array, axis):
    half = array.shape[0] // 2
    before, after = shift(array, axis, 1), shift(array, axis, -1)
    far = jnp.concatenate([shift(before[:half], axis, 1), shift(after[half:], axis, -1)], 0)
    return before, after, far


def ring_of_eight(array, axis):
    half = array.shape[0] // 2
    before = after = array
    held = [array]
    for _ in range(3):
        before, after = shift(before, axis, 1), shift(after, axis, -1)
        held += [after, before]
    held.append(jnp.concatenate([shift(before[:half], axis, 1), shift(after[half:], axis, -1)], 0))
    return held


def first_and_last(hit, keys, top):
    return jnp.stack(
        [jnp.min(jnp.where(hit, keys, top), -1), jnp.max(jnp.where(hit, keys, 0), -1)], -1
    )


def chunk_kernel(first, count, where, left_at, right_at, *refs):
    left, pieces, rights, out, tile = refs[0], refs[1:5], refs[5 : 5 + count], refs[-2], refs[-1]
    here = where[0]
    sources, terms = left.shape[0], left.shape[2]
    rows = pieces[0].shape[-2]
    size = left.shape[-1]

    def one_source(source, _):
        for step in range(count):
            for rank in range(CAP):
                slot = (source * len(STEPS) + first + step) * CAP + rank
                i, j = left_at[slot], right_at[slot]
                for away, piece in enumerate(pieces):
                    quarter = lax.rem(here + (0, 3, 1, 2)[away], 4)
                    tile[step * CAP + rank, pl.ds(pl.multiple_of(quarter * rows, rows), rows)] = (
                        piece[source, first + step, rank]
                    )
                psi = tile[step * CAP + rank]
                total = jnp.zeros((size, size), jnp.float32)
                for term in range(terms):
                    product = jnp.dot(
                        left[source, i, term], psi, preferred_element_type=jnp.float32
                    ).astype(jnp.bfloat16)
                    total += lax.dot_general(
                        product,
                        rights[step][j, term],
                        (((1,), (1,)), ((), ())),
                        preferred_element_type=jnp.float32,
                    )
                total = total.astype(jnp.bfloat16)
                for quarter in range(4):
                    out[quarter, source, step, rank] = total[quarter * rows : (quarter + 1) * rows]
        return 0

    lax.fori_loop(0, sources, one_source, 0)


def compute_chunk(first, count, where, left_at, right_at, left, pieces, rights):
    sources, _, terms, size, _ = left.shape
    rows = pieces[0].shape[-2]
    slots = sources * count * CAP
    smem = pl.BlockSpec(memory_space=pltpu.SMEM)
    vmem = pl.BlockSpec(memory_space=pltpu.VMEM)
    return pl.pallas_call(
        functools.partial(chunk_kernel, first, count),
        out_shape=jax.ShapeDtypeStruct((4, sources, count, CAP, rows, size), jnp.bfloat16),
        in_specs=[smem] * 3 + [vmem] * (5 + count),
        out_specs=vmem,
        scratch_shapes=[pltpu.VMEM((count * CAP, size, size), jnp.bfloat16)],
        compiler_params=pltpu.CompilerParams(vmem_limit_bytes=50 * 1024 * 1024),
        cost_estimate=pl.CostEstimate(
            flops=slots * terms * 4 * size**3 * 4,
            bytes_accessed=slots * size * size * 4,
            transcendentals=0,
        ),
    )(where, left_at, right_at, left, *pieces, *rights)


def on_device(wavefunction, left_env, right_env, left_dims, right_dims, partner):
    sectors, pairs, size, _ = wavefunction.shape
    tiles = sectors * pairs
    x, z, k, y = (lax.axis_index(name) for name in ("x", "z", "k", "y"))
    nx, nz, nk, ny = (lax.axis_size(name) for name in ("x", "z", "k", "y"))
    rows = size // ny
    steps = jnp.array(STEPS, jnp.int32)
    place = jnp.array([STEPS.index(d if d <= 4 else d - nz) for d in range(nz)], jnp.int32)

    left_all = lax.all_gather(jnp.swapaxes(left_env, 0, 1), ("x", "k"))
    rights = ring_of_eight(jnp.swapaxes(right_env, 0, 1), "z")

    block = (x * nz + z) * nk + k
    own_partner = lax.dynamic_slice_in_dim(partner, block * sectors, sectors, 0).reshape(tiles)
    own_dims = lax.dynamic_slice_in_dim(left_dims, block * sectors, sectors, 0)
    owner = own_partner // sectors
    order = jnp.arange(tiles, dtype=jnp.int32)
    zs = (z + steps) % nz
    xs, ks = jnp.arange(nx, dtype=jnp.int32), jnp.arange(nk, dtype=jnp.int32)
    targets = ((xs[:, None, None] * nz + zs) * nk + ks[:, None]).reshape(nx * nk * nz)
    sent = first_and_last(targets[:, None] == owner, order, tiles - 1).reshape(-1)
    columns = jnp.arange(size, dtype=jnp.int32)
    own_rows = lax.dynamic_slice_in_dim(columns, y * rows, rows)
    row_mask = (own_rows < jnp.repeat(own_dims, pairs)[:, None]).astype(jnp.bfloat16)
    column_mask = (columns < jnp.take(right_dims, own_partner)[:, None]).astype(jnp.bfloat16)
    mask = row_mask[:, :, None] * column_mask[:, None, :]
    quarter = lax.dynamic_slice_in_dim(wavefunction, y * rows, rows, 2).reshape(tiles, rows, size)
    outgoing = jnp.take(quarter * mask, sent, axis=0, mode="clip")
    incoming = lax.all_to_all(
        outgoing.reshape(nx * nk, nz, CAP, rows, size), ("x", "k"), 0, 0, tiled=True
    )
    pieces = (incoming, *both_ways(incoming, "y"))

    group = lax.dynamic_index_in_dim(partner.reshape(nx, nz, nk, tiles), z, 1, keepdims=False)
    group = group.reshape(nx * nk, 1, tiles)
    wanted = ((x * nz + zs) * nk + k)[None, :, None]
    keys = first_and_last(
        group // sectors == wanted, order * 8 + group % sectors, (tiles - 1) * 8 + sectors - 1
    ).reshape(-1)
    left_at, right_at = keys // (8 * pairs), jnp.minimum(keys % 8, sectors - 1)

    where = y.astype(jnp.int32).reshape(1)
    parts = []
    for first, last in CHUNKS:
        partial = compute_chunk(
            first, last - first, where, left_at, right_at, left_all, pieces, rights[first:last]
        )
        shares = lax.all_to_all(partial, "y", 0, 0, tiled=True)
        parts.append(jnp.sum(shares.astype(jnp.float32), 0).astype(jnp.bfloat16))
    finished = jnp.concatenate(parts, 1)
    returned = lax.all_to_all(finished, ("x", "k"), 0, 0, tiled=True)
    returned = returned.reshape(nx * nk * nz * CAP, rows, size)

    lane = owner // (nz * nk) * nk + owner % nk
    again = jnp.any((owner[None, :] == owner[:, None]) & (order[None, :] < order[:, None]), 1)
    spot = (lane * nz + jnp.take(place, (owner // nk - z) % nz)) * CAP + again.astype(jnp.int32)
    own = jnp.take(returned, spot, axis=0, mode="clip") * mask
    return own.reshape(sectors, pairs, rows, size)


def solution(mesh):
    fine = Mesh(mesh.devices.reshape(4, 8, 2, 4), ("x", "z", "k", "y"))
    blk = ("x", "z", "k")
    placed = (P(blk), P("y", blk), P("y", blk), P(), P(), P())
    return jax.shard_map(
        on_device, mesh=fine, in_specs=placed, out_specs=P(blk, None, "y", None), check_vma=False
    )
```

```python
import functools

import jax
import jax.numpy as jnp
from jax import lax
from jax.experimental import pallas as pl
from jax.experimental.pallas import tpu as pltpu
from jax.sharding import Mesh
from jax.sharding import PartitionSpec as P

STEPS = (0, 1, -1, 2, -2, 3, -3, 4)
EARLY = 3
CAP = 2
MIB = 1024 * 1024
SMEM = pl.BlockSpec(memory_space=pltpu.SMEM)
VMEM = pl.BlockSpec(memory_space=pltpu.VMEM)
ANY = pl.BlockSpec(memory_space=pl.ANY)
CLOCK = 5 * 10**9


def shift(array, axis, by):
    count = lax.axis_size(axis)
    return lax.ppermute(array, axis, [(i, (i + by) % count) for i in range(count)])


def hold(*refs):
    pass


def after_these(arrays, others, flops=0):
    return pl.pallas_call(
        hold,
        out_shape=[jax.ShapeDtypeStruct(a.shape, a.dtype) for a in arrays],
        in_specs=[ANY] * (len(arrays) + len(others)),
        out_specs=[ANY] * len(arrays),
        input_output_aliases={i: i for i in range(len(arrays))},
        cost_estimate=pl.CostEstimate(flops=flops, bytes_accessed=0, transcendentals=0),
    )(*arrays, *others)


def first_and_last(hit, keys, top):
    return jnp.stack(
        [jnp.min(jnp.where(hit, keys, top), -1), jnp.max(jnp.where(hit, keys, 0), -1)], -1
    )


def slot_of(tile, partner, place, seen, z):
    owner = lax.div(partner[tile], 6)
    lane = (owner >> 4) * 2 + (owner & 1)
    step = place[((owner >> 1) - z) & 7]
    rank = seen[owner]
    seen[owner] = rank + 1
    return lane, step, rank


def clear(seen):
    def one(i, _):
        seen[i] = 0
        return 0

    lax.fori_loop(0, seen.shape[0], one, 0)


def send_kernel(spot, place, partner, left_dims, right_dims, psi, early, late, seen):
    z, y = spot[0], spot[1]
    tiles, size, _ = psi.shape
    rows = early.shape[-2]
    pairs = tiles // left_dims.shape[0]
    row = lax.broadcasted_iota(jnp.int32, (size, size), 0)
    column = lax.broadcasted_iota(jnp.int32, (size, size), 1)
    start = pl.multiple_of(y * rows, rows)
    clear(seen)

    def one_tile(tile, _):
        lane, step, rank = slot_of(tile, partner, place, seen, z)
        height, width = left_dims[lax.div(tile, pairs)], right_dims[partner[tile]]

        @pl.when(step < EARLY)
        def _():
            keep = (row[:rows] < height - start) & (column[:rows] < width)
            values = psi[tile, pl.ds(start, rows)].astype(jnp.float32)
            early[lane, step, rank] = jnp.where(keep, values, 0.0).astype(psi.dtype)

        @pl.when(step >= EARLY)
        def _():
            keep = (row < height) & (column < width)
            values = psi[tile].astype(jnp.float32)
            late[lane, step - EARLY, rank] = jnp.where(keep, values, 0.0).astype(psi.dtype)

        return 0

    lax.fori_loop(0, tiles, one_tile, 0)


def chunk_kernel(first, count, begin, quarters, halves, relative, spot, left_at, right_at, *refs):
    refs = list(refs)
    lefts = [refs.pop(0) for _ in range(8)]
    sent = [refs.pop(0) for _ in range(quarters)]
    rights = [[refs.pop(0) for _ in range(parts)] for parts in halves]
    out, left, right, psi, total, flags = refs[-6:]
    x, y, k = spot[3], spot[1], spot[2]
    terms, size = left.shape[1], left.shape[-1]
    rows = size // 4
    copies = []

    def copy(source, there):
        copies.append(pltpu.make_async_copy(source, there, flags.at[len(copies)]))
        copies[-1].start()

    for step, parts in enumerate(rights):
        start = 0
        for part in parts:
            copy(part, right.at[step, pl.ds(start, part.shape[0])])
            start += part.shape[0]
    for away, part in enumerate(sent):
        if quarters == 4:
            row = pl.multiple_of(lax.rem(y + away, 4) * rows, rows)
            copy(part, psi.at[:, :, :, pl.ds(row, rows)])
        else:
            copy(part.at[:, pl.ds(begin, count)], psi)
    groups = ((0, 2), (2, 8))
    for low, high in groups:
        for away in range(low, high):
            copy(lefts[away], left.at[away])
    for ready in copies[:-8]:
        ready.wait()
    for low, high in groups:
        for away in range(low, high):
            copies[-8:][away].wait()
        for away in range(low, high):
            lane = lax.rem(x + away // 2, 4) * 2 + (k if away % 2 == 0 else 1 - k)
            for step in range(count):
                for rank in range(CAP):
                    slot = (lane * len(STEPS) + first + step) * CAP + rank
                    i, j = left_at[slot], right_at[slot]
                    stack = jnp.concatenate([left[away, term, i] for term in range(terms)], 0)
                    product = jnp.dot(
                        stack, psi[lane, step, rank], preferred_element_type=jnp.float32
                    ).astype(jnp.bfloat16)
                    side = [product[term * size : (term + 1) * size] for term in range(terms)]
                    other = jnp.concatenate([right[step, term, j] for term in range(terms)], 1)
                    total[lane, step, rank] = lax.dot_general(
                        jnp.concatenate(side, 1),
                        other,
                        (((1,), (1,)), ((), ())),
                        preferred_element_type=jnp.float32,
                    ).astype(jnp.bfloat16)
    copies.clear()
    for far in range(4):
        quarter = lax.rem(y + far, 4) if relative else far
        row = pl.multiple_of(quarter * rows, rows)
        copy(total.at[:, :, :, pl.ds(row, rows)], out.at[far])
    for ready in copies:
        ready.wait()


def compute_chunk(first, count, begin, spot, left_at, right_at, lefts, sent, rights, after, relative):
    sources = len(lefts)
    terms, sectors, size, _ = lefts[0].shape
    rows, slots = size // 4, sources * count * CAP
    quarters, halves = len(sent), [len(parts) for parts in rights]
    flat = [part for parts in rights for part in parts]
    return pl.pallas_call(
        functools.partial(chunk_kernel, first, count, begin, quarters, halves, relative),
        out_shape=jax.ShapeDtypeStruct((4, sources, count, CAP, rows, size), jnp.bfloat16),
        in_specs=[SMEM] * 3 + [ANY] * (8 + quarters + len(flat) + len(after)),
        out_specs=ANY,
        scratch_shapes=[
            pltpu.VMEM((sources, terms, sectors, size, size), jnp.bfloat16),
            pltpu.VMEM((count, terms, sectors, size, size), jnp.bfloat16),
            pltpu.VMEM((sources, count, CAP, size, size), jnp.bfloat16),
            pltpu.VMEM((sources, count, CAP, size, size), jnp.bfloat16),
            pltpu.SemaphoreType.DMA((8 + quarters + len(flat),)),
        ],
        compiler_params=pltpu.CompilerParams(vmem_limit_bytes=56 * MIB),
        cost_estimate=pl.CostEstimate(
            flops=slots * terms * 4 * size**3 * 6,
            bytes_accessed=slots * size * size * 4,
            transcendentals=0,
        ),
    )(spot, left_at, right_at, *lefts, *sent, *flat, *after)


def finish_kernel(spot, place, partner, left_dims, right_dims, *refs):
    parts, (out, seen) = refs[:2], refs[2:]
    z, y = spot[0], spot[1]
    tiles, rows, size = out.shape
    pairs = tiles // left_dims.shape[0]
    row = lax.broadcasted_iota(jnp.int32, (rows, size), 0) + y * rows
    column = lax.broadcasted_iota(jnp.int32, (rows, size), 1)
    clear(seen)

    def one_tile(tile, _):
        lane, step, rank = slot_of(tile, partner, place, seen, z)
        keep = (row < left_dims[lax.div(tile, pairs)]) & (column < right_dims[partner[tile]])
        start = 0
        for part in parts:
            planes, count = part.shape[0] // 8, part.shape[1]

            @pl.when((step >= start) & (step < start + count))
            def _(part=part, planes=planes, start=start):
                whole = part[lane, step - start, rank].astype(jnp.float32)
                for plane in range(1, planes):
                    whole += part[plane * 8 + lane, step - start, rank].astype(jnp.float32)
                out[tile] = jnp.where(keep, whole, 0.0).astype(out.dtype)

            start += count
        return 0

    lax.fori_loop(0, tiles, one_tile, 0)


def on_device(wavefunction, left_env, right_env, left_dims, right_dims, partner):
    sectors, pairs, size, _ = wavefunction.shape
    tiles = sectors * pairs
    x, z, k, y = (lax.axis_index(name) for name in ("x", "z", "k", "y"))
    nx, nz, nk, ny = (lax.axis_size(name) for name in ("x", "z", "k", "y"))
    rows, lanes, many = size // ny, nx * nk, len(STEPS)
    steps = jnp.array(STEPS, jnp.int32)
    place = jnp.array([STEPS.index(d if d <= 4 else d - nz) for d in range(nz)], jnp.int32)
    spot = jnp.stack([z, y, k, x]).astype(jnp.int32)

    def both_ways(arrays):
        return shift(arrays[0], "z", 1), shift(arrays[1], "z", -1)

    one = both_ways((right_env, right_env))
    block = (x * nz + z) * nk + k
    own_partner = lax.dynamic_slice_in_dim(partner, block * sectors, sectors, 0).reshape(tiles)
    own_dims = lax.dynamic_slice_in_dim(left_dims, block * sectors, sectors, 0)
    own = (spot, place, own_partner, own_dims, right_dims)
    counters = [pltpu.SMEM((nx * nz * nk,), jnp.int32)]
    early, late = pl.pallas_call(
        send_kernel,
        out_shape=[
            jax.ShapeDtypeStruct((lanes, EARLY, CAP, rows, size), jnp.bfloat16),
            jax.ShapeDtypeStruct((lanes, many - EARLY, CAP, size, size), jnp.bfloat16),
        ],
        in_specs=[SMEM] * 5 + [VMEM],
        out_specs=[VMEM, VMEM],
        scratch_shapes=counters,
        compiler_params=pltpu.CompilerParams(vmem_limit_bytes=20 * MIB),
    )(*own, wavefunction.reshape(tiles, size, size))
    one = after_these(one, (early, late), CLOCK)
    two = both_ways(one)
    after, before = shift(left_env, "x", -1), shift(left_env, "x", 1)
    lefts = [left_env, after, shift(before, "x", 1), before]
    lefts = [both for own in lefts for both in (own, shift(own, "k", 1))]
    early = lax.all_to_all(early, ("x", "k"), 0, 0, tiled=True)
    late = [lax.all_to_all(late, ("x", "k"), 0, 0, tiled=True)]
    (early,) = after_these((early,), (*one, lefts[3], lefts[7]))
    after, before = shift(early, "y", -1), shift(early, "y", 1)
    two = after_these(two, (after, before, lefts[1]), CLOCK)
    three = both_ways(two)
    early = [early, after, shift(before, "y", 1), before]

    group = lax.dynamic_index_in_dim(partner.reshape(nx, nz, nk, tiles), z, 1, keepdims=False)
    group = group.reshape(lanes, 1, tiles)
    order = jnp.arange(tiles, dtype=jnp.int32)
    wanted = ((x * nz + (z + steps) % nz) * nk + k)[None, :, None]
    keys = first_and_last(
        group // sectors == wanted, order * 8 + group % sectors, (tiles - 1) * 8 + sectors - 1
    ).reshape(-1)
    left_at, right_at = keys // (8 * pairs), jnp.minimum(keys % 8, sectors - 1)

    def chunk(first, stop, sent, after, relative=False):
        begin = 0 if first < EARLY else first - EARLY
        return compute_chunk(
            first, stop - first, begin, spot, left_at, right_at, lefts, sent, rights[first:stop], after, relative
        )

    def straight_back(partial):
        partial = partial.reshape(ny * lanes, *partial.shape[2:])
        return lax.all_to_all(partial, ("y", "x", "k"), 0, 0, tiled=True)

    rights = [[right_env], *[[two_way] for two_way in (one[1], one[0])]]
    first = chunk(0, EARLY, early, [*two])
    three = after_these(three, (first,), CLOCK)
    half = right_env.shape[0] // 2
    four = both_ways((three[0][:half], three[1][half:]))
    (held,) = after_these((first,), late)
    first_back = straight_back(held)
    rights += [[two[1]], [two[0]], [three[1]], [three[0]], [*four]]
    second = chunk(EARLY, many, late, [first])
    second_back = straight_back(second)
    out = pl.pallas_call(
        finish_kernel,
        out_shape=jax.ShapeDtypeStruct((tiles, rows, size), jnp.bfloat16),
        in_specs=[SMEM] * 5 + [VMEM] * 2,
        out_specs=VMEM,
        scratch_shapes=counters,
        compiler_params=pltpu.CompilerParams(vmem_limit_bytes=20 * MIB),
    )(*own, first_back, second_back)
    return out.reshape(sectors, pairs, rows, size)


def solution(mesh):
    fine = Mesh(mesh.devices.reshape(4, 8, 2, 4), ("x", "z", "k", "y"))
    blk = ("x", "z", "k")
    placed = (P(blk), P("y", blk), P("y", blk), P(), P(), P())
    return jax.shard_map(
        on_device, mesh=fine, in_specs=placed, out_specs=P(blk, None, "y", None), check_vma=False
    )
```

```python
import functools

import jax
import jax.numpy as jnp
from jax import lax
from jax.experimental import pallas as pl
from jax.experimental.pallas import tpu as pltpu
from jax.sharding import Mesh
from jax.sharding import PartitionSpec as P

STEPS = (0, 1, -1, 2, -2, 3, -3, 4)
EARLY = 3
CAP = 2
MIB = 1024 * 1024
SMEM = pl.BlockSpec(memory_space=pltpu.SMEM)
VMEM = pl.BlockSpec(memory_space=pltpu.VMEM)
ANY = pl.BlockSpec(memory_space=pl.ANY)
CLOCK = 5 * 10**9


def shift(array, axis, by):
    count = lax.axis_size(axis)
    return lax.ppermute(array, axis, [(i, (i + by) % count) for i in range(count)])


def hold(*refs):
    pass


def after_these(arrays, others, flops=0):
    return pl.pallas_call(
        hold,
        out_shape=[jax.ShapeDtypeStruct(a.shape, a.dtype) for a in arrays],
        in_specs=[ANY] * (len(arrays) + len(others)),
        out_specs=[ANY] * len(arrays),
        input_output_aliases={i: i for i in range(len(arrays))},
        cost_estimate=pl.CostEstimate(flops=flops, bytes_accessed=0, transcendentals=0),
    )(*arrays, *others)


def first_and_last(hit, keys, top):
    return jnp.stack(
        [jnp.min(jnp.where(hit, keys, top), -1), jnp.max(jnp.where(hit, keys, 0), -1)], -1
    )


def slot_of(tile, partner, place, seen, z):
    owner = lax.div(partner[tile], 6)
    lane = (owner >> 4) * 2 + (owner & 1)
    step = place[((owner >> 1) - z) & 7]
    rank = seen[owner]
    seen[owner] = rank + 1
    return lane, step, rank


def clear(seen):
    def one(i, _):
        seen[i] = 0
        return 0

    lax.fori_loop(0, seen.shape[0], one, 0)


def send_kernel(spot, place, partner, left_dims, right_dims, psi, early, late, seen):
    z, y = spot[0], spot[1]
    tiles, size, _ = psi.shape
    rows = early.shape[-2]
    pairs = tiles // left_dims.shape[0]
    row = lax.broadcasted_iota(jnp.int32, (size, size), 0)
    column = lax.broadcasted_iota(jnp.int32, (size, size), 1)
    start = pl.multiple_of(y * rows, rows)
    clear(seen)

    def one_tile(tile, _):
        lane, step, rank = slot_of(tile, partner, place, seen, z)
        height, width = left_dims[lax.div(tile, pairs)], right_dims[partner[tile]]

        @pl.when(step < EARLY)
        def _():
            keep = (row[:rows] < height - start) & (column[:rows] < width)
            values = psi[tile, pl.ds(start, rows)].astype(jnp.float32)
            early[lane, step, rank] = jnp.where(keep, values, 0.0).astype(psi.dtype)

        @pl.when(step >= EARLY)
        def _():
            keep = (row < height) & (column < width)
            values = psi[tile].astype(jnp.float32)
            late[lane, step - EARLY, rank] = jnp.where(keep, values, 0.0).astype(psi.dtype)

        return 0

    lax.fori_loop(0, tiles, one_tile, 0)


def chunk_kernel(first, count, begin, quarters, halves, relative, spot, left_at, right_at, *refs):
    refs = list(refs)
    lefts = [refs.pop(0) for _ in range(8)]
    sent = [refs.pop(0) for _ in range(quarters)]
    rights = [[refs.pop(0) for _ in range(parts)] for parts in halves]
    out, left, right, psi, total, flags = refs[-6:]
    x, y, k = spot[3], spot[1], spot[2]
    terms, size = left.shape[1], left.shape[-1]
    rows = size // 4
    copies = []

    def copy(source, there):
        copies.append(pltpu.make_async_copy(source, there, flags.at[len(copies)]))
        copies[-1].start()

    for step, parts in enumerate(rights):
        start = 0
        for part in parts:
            copy(part, right.at[step, pl.ds(start, part.shape[0])])
            start += part.shape[0]
    for away, part in enumerate(sent):
        if quarters == 4:
            row = pl.multiple_of(lax.rem(y + away, 4) * rows, rows)
            copy(part, psi.at[:, :, :, pl.ds(row, rows)])
        else:
            copy(part.at[:, pl.ds(begin, count)], psi)
    groups = ((0, 2), (2, 8))
    for low, high in groups:
        for away in range(low, high):
            copy(lefts[away], left.at[away])
    for ready in copies[:-8]:
        ready.wait()
    for low, high in groups:
        for away in range(low, high):
            copies[-8:][away].wait()
        for away in range(low, high):
            lane = lax.rem(x + away // 2, 4) * 2 + (k if away % 2 == 0 else 1 - k)
            for step in range(count):
                for rank in range(CAP):
                    slot = (lane * len(STEPS) + first + step) * CAP + rank
                    i, j = left_at[slot], right_at[slot]
                    stack = jnp.concatenate([left[away, term, i] for term in range(terms)], 0)
                    product = jnp.dot(
                        stack, psi[lane, step, rank], preferred_element_type=jnp.float32
                    ).astype(jnp.bfloat16)
                    side = [product[term * size : (term + 1) * size] for term in range(terms)]
                    other = jnp.concatenate([right[step, term, j] for term in range(terms)], 1)
                    total[lane, step, rank] = lax.dot_general(
                        jnp.concatenate(side, 1),
                        other,
                        (((1,), (1,)), ((), ())),
                        preferred_element_type=jnp.float32,
                    ).astype(jnp.bfloat16)
    copies.clear()
    for far in range(4):
        quarter = lax.rem(y + far, 4) if relative else far
        row = pl.multiple_of(quarter * rows, rows)
        copy(total.at[:, :, :, pl.ds(row, rows)], out.at[:, far])
    for ready in copies:
        ready.wait()


def compute_chunk(first, count, begin, spot, left_at, right_at, lefts, sent, rights, after, relative):
    sources = len(lefts)
    terms, sectors, size, _ = lefts[0].shape
    rows, slots = size // 4, sources * count * CAP
    quarters, halves = len(sent), [len(parts) for parts in rights]
    flat = [part for parts in rights for part in parts]
    return pl.pallas_call(
        functools.partial(chunk_kernel, first, count, begin, quarters, halves, relative),
        out_shape=jax.ShapeDtypeStruct((sources, 4, count, CAP, rows, size), jnp.bfloat16),
        in_specs=[SMEM] * 3 + [ANY] * (8 + quarters + len(flat) + len(after)),
        out_specs=ANY,
        scratch_shapes=[
            pltpu.VMEM((sources, terms, sectors, size, size), jnp.bfloat16),
            pltpu.VMEM((count, terms, sectors, size, size), jnp.bfloat16),
            pltpu.VMEM((sources, count, CAP, size, size), jnp.bfloat16),
            pltpu.VMEM((sources, count, CAP, size, size), jnp.bfloat16),
            pltpu.SemaphoreType.DMA((8 + quarters + len(flat),)),
        ],
        compiler_params=pltpu.CompilerParams(vmem_limit_bytes=56 * MIB),
        cost_estimate=pl.CostEstimate(
            flops=slots * terms * 4 * size**3 * 6,
            bytes_accessed=slots * size * size * 4,
            transcendentals=0,
        ),
    )(spot, left_at, right_at, *lefts, *sent, *flat, *after)


def finish_kernel(spot, place, partner, left_dims, right_dims, *refs):
    parts, (out, seen) = refs[:2], refs[2:]
    z, y = spot[0], spot[1]
    tiles, rows, size = out.shape
    pairs = tiles // left_dims.shape[0]
    row = lax.broadcasted_iota(jnp.int32, (rows, size), 0) + y * rows
    column = lax.broadcasted_iota(jnp.int32, (rows, size), 1)
    clear(seen)

    def one_tile(tile, _):
        lane, step, rank = slot_of(tile, partner, place, seen, z)
        keep = (row < left_dims[lax.div(tile, pairs)]) & (column < right_dims[partner[tile]])
        start = 0
        for part in parts:
            planes, count = part.shape[0] // 8, part.shape[1]

            @pl.when((step >= start) & (step < start + count))
            def _(part=part, planes=planes, start=start):
                whole = part[lane * planes, step - start, rank].astype(jnp.float32)
                for plane in range(1, planes):
                    whole += part[lane * planes + plane, step - start, rank].astype(jnp.float32)
                out[tile] = jnp.where(keep, whole, 0.0).astype(out.dtype)

            start += count
        return 0

    lax.fori_loop(0, tiles, one_tile, 0, unroll=4)


def on_device(wavefunction, left_env, right_env, left_dims, right_dims, partner):
    sectors, pairs, size, _ = wavefunction.shape
    tiles = sectors * pairs
    x, z, k, y = (lax.axis_index(name) for name in ("x", "z", "k", "y"))
    nx, nz, nk, ny = (lax.axis_size(name) for name in ("x", "z", "k", "y"))
    rows, lanes, many = size // ny, nx * nk, len(STEPS)
    steps = jnp.array(STEPS, jnp.int32)
    place = jnp.array([STEPS.index(d if d <= 4 else d - nz) for d in range(nz)], jnp.int32)
    spot = jnp.stack([z, y, k, x]).astype(jnp.int32)

    def both_ways(arrays):
        return shift(arrays[0], "z", 1), shift(arrays[1], "z", -1)

    one = both_ways((right_env, right_env))
    block = (x * nz + z) * nk + k
    own_partner = lax.dynamic_slice_in_dim(partner, block * sectors, sectors, 0).reshape(tiles)
    own_dims = lax.dynamic_slice_in_dim(left_dims, block * sectors, sectors, 0)
    own = (spot, place, own_partner, own_dims, right_dims)
    counters = [pltpu.SMEM((nx * nz * nk,), jnp.int32)]
    early, late = pl.pallas_call(
        send_kernel,
        out_shape=[
            jax.ShapeDtypeStruct((lanes, EARLY, CAP, rows, size), jnp.bfloat16),
            jax.ShapeDtypeStruct((lanes, many - EARLY, CAP, size, size), jnp.bfloat16),
        ],
        in_specs=[SMEM] * 5 + [VMEM],
        out_specs=[VMEM, VMEM],
        scratch_shapes=counters,
        compiler_params=pltpu.CompilerParams(vmem_limit_bytes=20 * MIB),
    )(*own, wavefunction.reshape(tiles, size, size))
    one = after_these(one, (early, late), CLOCK)
    two = both_ways(one)
    after, before = shift(left_env, "x", -1), shift(left_env, "x", 1)
    lefts = [left_env, after, shift(before, "x", 1), before]
    lefts = [both for own in lefts for both in (own, shift(own, "k", 1))]
    early = lax.all_to_all(early, ("x", "k"), 0, 0, tiled=True)
    late = [lax.all_to_all(late, ("x", "k"), 0, 0, tiled=True)]
    (early,) = after_these((early,), (*one, lefts[3], lefts[7]))
    after, before = shift(early, "y", -1), shift(early, "y", 1)
    two = after_these(two, (after, before, lefts[1]), CLOCK)
    three = both_ways(two)
    early = [early, after, shift(before, "y", 1), before]

    group = lax.dynamic_index_in_dim(partner.reshape(nx, nz, nk, tiles), z, 1, keepdims=False)
    group = group.reshape(lanes, 1, tiles)
    order = jnp.arange(tiles, dtype=jnp.int32)
    wanted = ((x * nz + (z + steps) % nz) * nk + k)[None, :, None]
    keys = first_and_last(
        group // sectors == wanted, order * 8 + group % sectors, (tiles - 1) * 8 + sectors - 1
    ).reshape(-1)
    left_at, right_at = keys // (8 * pairs), jnp.minimum(keys % 8, sectors - 1)

    def chunk(first, stop, sent, after, relative=False):
        begin = 0 if first < EARLY else first - EARLY
        return compute_chunk(
            first, stop - first, begin, spot, left_at, right_at, lefts, sent, rights[first:stop], after, relative
        )

    def straight_back(partial):
        partial = partial.reshape(ny * lanes, *partial.shape[2:])
        return lax.all_to_all(partial, ("x", "k", "y"), 0, 0, tiled=True)

    rights = [[right_env], *[[two_way] for two_way in (one[1], one[0])]]
    first = chunk(0, EARLY, early, [*two])
    three = after_these(three, (first,), CLOCK)
    half = right_env.shape[0] // 2
    four = both_ways((three[0][:half], three[1][half:]))
    (held,) = after_these((first,), late)
    first_back = straight_back(held)
    rights += [[two[1]], [two[0]], [three[1]], [three[0]], [*four]]
    second = chunk(EARLY, many, late, [first])
    second_back = straight_back(second)
    out = pl.pallas_call(
        finish_kernel,
        out_shape=jax.ShapeDtypeStruct((tiles, rows, size), jnp.bfloat16),
        in_specs=[SMEM] * 5 + [VMEM] * 2,
        out_specs=VMEM,
        scratch_shapes=counters,
        compiler_params=pltpu.CompilerParams(vmem_limit_bytes=20 * MIB),
    )(*own, first_back, second_back)
    return out.reshape(sectors, pairs, rows, size)


def solution(mesh):
    fine = Mesh(mesh.devices.reshape(4, 8, 2, 4), ("x", "z", "k", "y"))
    blk = ("x", "z", "k")
    placed = (P(blk), P("y", blk), P("y", blk), P(), P(), P())
    return jax.shard_map(
        on_device, mesh=fine, in_specs=placed, out_specs=P(blk, None, "y", None), check_vma=False
    )
```
